32 devices in a mesh: row: 4 (over x, core), col: 8 (over z, y).
Axes of the slice: x: 2, y: 2, z: 4, core: 2. Of those that a mesh axis runs over, the one named last changes fastest.
Arguments:
- tokens: bfloat16 [128, 8192], P('col', 'row'), may hold values from -6 to 6
- out_grad: bfloat16 [128, 8192], P('col', 'row'), may hold values from -2 to 2
- gate_weight: bfloat16 [8192, 28672], P('row', 'col'), may hold values from -0.0625 to 0.0625
- up_weight: bfloat16 [8192, 28672], P('row', 'col'), may hold values from -0.0625 to 0.0625
- down_weight: bfloat16 [28672, 8192], P('col', 'row'), may hold values from -0.03125 to 0.03125
Outputs:
- grad_input: bfloat16 [128, 8192], P('col', 'row')
- grad_gate: bfloat16 [8192, 28672], P('row', 'col')
- grad_up: bfloat16 [8192, 28672], P('row', 'col')
- grad_down: bfloat16 [28672, 8192], P('col', 'row')
The draws below stay inside these ranges and needn't reach their ends.
All inputs are finite; a program needn't handle non-finite values.
Results may differ from the reference program's by a relative error of at most 0.005.
Values may be sent and summed in bfloat16 or wider, within the bound.
A program may use at most 128 MiB of HBM per device.

```python
import jax
import jax.numpy as jnp
from jax import lax

D = 8192
FF = 28672
TOKENS = 128
N_COL = 8


def block_scale(key, extent, shards, smallest, high):
    def one(position, blocks):
        steps = jax.random.uniform(jax.random.fold_in(jax.random.fold_in(key, 6), position), (blocks,), jnp.float32, smallest / len(shards), high / len(shards))
        return jnp.repeat(jnp.exp(steps), extent[position] // blocks).reshape((-1,) + (1,) * (len(extent) - position - 1))

    loudness = one(*shards[0])
    for cut in shards[1:]:
        loudness = loudness * one(*cut)
    return loudness


def gaussian(own_key, dims, deviation, most, shards=(), held_as=jnp.bfloat16):
    result = deviation * jax.random.normal(own_key, dims, jnp.float32)
    if shards:
        result = result * block_scale(own_key, dims, shards, -0.22, 0.18)
    return jnp.clip(result, -most, most).astype(held_as)


def setup_inputs(seed: int = 0) -> dict:
    key_list = jax.random.split(jax.random.key(seed), 6)
    tokens = gaussian(key_list[0], (TOKENS, D), 1.0, 6.0, ((0, 8), (1, 4)))
    out_grad = gaussian(key_list[1], (TOKENS, D), 0.15, 2.0, ((0, 8), (1, 4)))
    gate_weight = gaussian(key_list[2], (D, FF), D ** -0.5, 0.0625, ((0, 4), (1, 8)))
    up_weight = gaussian(key_list[3], (D, FF), D ** -0.5, 0.0625, ((0, 4), (1, 8)))
    down_weight = gaussian(key_list[4], (FF, D), FF ** -0.5, 0.03125, ((0, 8), (1, 4)))
    return dict(tokens=tokens, out_grad=out_grad, gate_weight=gate_weight, up_weight=up_weight, down_weight=down_weight)


def pointwise(gate, up, hidden_grad):
    logistic = jax.nn.sigmoid(gate)
    active = gate * logistic
    hidden = (active * up).astype(jnp.bfloat16)
    d_gate = (hidden_grad * up * logistic * (1.0 + gate * (1.0 - logistic))).astype(jnp.bfloat16)
    d_up = (hidden_grad * active).astype(jnp.bfloat16)
    return hidden, d_gate, d_up


def reference(tokens, out_grad, gate_weight, up_weight, down_weight):
    width = FF // N_COL
    gate_blocks = gate_weight.reshape(D, N_COL, width).transpose(1, 0, 2)
    up_blocks = up_weight.reshape(D, N_COL, width).transpose(1, 0, 2)
    down_blocks = down_weight.reshape(N_COL, width, D)

    def step(carry, pieces):
        gate_piece, up_piece, down_piece = pieces
        gate = jnp.dot(tokens, gate_piece, preferred_element_type=jnp.float32)
        up = jnp.dot(tokens, up_piece, preferred_element_type=jnp.float32)
        hidden_grad = jnp.dot(out_grad, down_piece.T, preferred_element_type=jnp.float32)
        hidden, d_gate, d_up = pointwise(gate, up, hidden_grad)
        grad_down = jnp.dot(hidden.T, out_grad, preferred_element_type=jnp.float32).astype(jnp.bfloat16)
        grad_gate = jnp.dot(tokens.T, d_gate, preferred_element_type=jnp.float32).astype(jnp.bfloat16)
        grad_up = jnp.dot(tokens.T, d_up, preferred_element_type=jnp.float32).astype(jnp.bfloat16)
        carry = carry + jnp.dot(d_gate, gate_piece.T, preferred_element_type=jnp.float32)
        carry = carry + jnp.dot(d_up, up_piece.T, preferred_element_type=jnp.float32)
        return carry, (grad_gate, grad_up, grad_down)

    initial = jnp.zeros((TOKENS, D), jnp.float32)
    total, stacked = lax.scan(step, initial, (gate_blocks, up_blocks, down_blocks))
    grad_gate = stacked[0].transpose(1, 0, 2).reshape(D, FF)
    grad_up = stacked[1].transpose(1, 0, 2).reshape(D, FF)
    grad_down = stacked[2].reshape(FF, D)
    return total.astype(jnp.bfloat16), grad_gate, grad_up, grad_down
```

```python
import functools

import jax
import jax.numpy as jnp
from jax import lax
from jax.experimental import pallas as pl
from jax.experimental.pallas import tpu as pltpu
from jax.sharding import PartitionSpec as P

MESH = pl.DeviceIdType.MESH
F32, BF16 = jnp.float32, jnp.bfloat16


def pointwise(gate, up, hidden_grad):
    logistic = jax.nn.sigmoid(gate)
    active = gate * logistic
    hidden = (active * up).astype(BF16)
    d_gate = (hidden_grad * up * logistic * (1.0 + gate * (1.0 - logistic))).astype(BF16)
    d_up = (hidden_grad * active).astype(BF16)
    return hidden, d_gate, d_up


def contract_last(left, right):
    return lax.dot_general(left, right, (((1,), (1,)), ((), ())), preferred_element_type=F32)


def chunk_width(units):
    for width in (512, 256, 128):
        if units % width == 0:
            return width
    return units


def loop(low, high, body):
    def step(index, carry):
        body(index)
        return carry

    lax.fori_loop(low, high, step, 0)


def forward_kernel(
    n, group, chunks, width,
    tokens, out_grad, gate_w, up_w, down_w,
    tok_out, grad_out, hid_out, dgate_out, dup_out, *rest,
):
    partial_outs = rest[:n]
    (
        tok, grad, wg, wu, wd, part, core_in, x_send, x_in, res, acc,
        w_sem, own_sem, ag_send, ag_fwd, ag_recv,
        core_send_sem, core_recv_sem, x_send_sem, x_recv_sem, res_send_sem, res_recv_sem,
        out_sem, full_sem,
    ) = rest[n:]
    block = tokens.shape[0]
    total = block * n
    half = total // 2
    row, me = lax.axis_index("row"), lax.axis_index("col")
    core = lax.rem(row, 2)
    core_peer = row + 1 - 2 * core
    x_peer = lax.rem(row + 2, 4)
    groups = n // group
    hi, lo = me // group, lax.rem(me, group)
    mine = pl.ds(pl.multiple_of(core * half, half), half)
    theirs = pl.ds(pl.multiple_of((1 - core) * half, half), half)

    def columns(c):
        return pl.ds(pl.multiple_of(c * width, width), width)

    def weight_copy(m, c):
        if m == 2:
            return pltpu.make_async_copy(
                down_w.at[columns(c), :], wd.at[columns(c), :], w_sem.at[m, c]
            )
        source, target = ((gate_w, wg), (up_w, wu))[m]
        return pltpu.make_async_copy(
            source.at[:, columns(c)], target.at[:, columns(c)], w_sem.at[m, c]
        )

    def load_pair(c):
        weight_copy(0, c).start()
        weight_copy(1, c).start()

    def place(owner):
        return pl.ds(pl.multiple_of(owner * block, block), block)

    def far(k):
        return lax.rem(hi + k, groups) * group + lo

    def far_from(k):
        return lax.rem(hi + groups - k, groups) * group + lo

    def near(j):
        return hi * group + lax.rem(lo + j, group)

    arrays = ((tokens, tok), (out_grad, grad))

    def own_copy(a):
        return pltpu.make_async_copy(arrays[a][0], arrays[a][1].at[place(me), :], own_sem.at[a])

    def own_send(a, peer):
        return pltpu.make_async_remote_copy(
            src_ref=arrays[a][0],
            dst_ref=arrays[a][1].at[place(me), :],
            send_sem=ag_send.at[a, peer],
            recv_sem=ag_recv.at[a, me],
            device_id={"col": peer},
            device_id_type=MESH,
        )

    def forward_send(a, owner, j):
        return pltpu.make_async_remote_copy(
            src_ref=arrays[a][1].at[place(owner), :],
            dst_ref=arrays[a][1].at[place(owner), :],
            send_sem=ag_fwd.at[a, owner, j],
            recv_sem=ag_recv.at[a, owner],
            device_id={"col": near(j)},
            device_id_type=MESH,
        )

    def wait_block(a, owner):
        pltpu.make_async_copy(
            arrays[a][0], arrays[a][1].at[place(owner), :], ag_recv.at[a, owner]
        ).wait()

    def gather_start(a):
        own_copy(a).start()
        loop(1, groups, lambda k: own_send(a, far(k)).start())
        loop(1, group, lambda j: own_send(a, near(j)).start())

    def gather_forward(a):
        def one(k):
            owner = far_from(k)
            wait_block(a, owner)
            loop(1, group, lambda j: forward_send(a, owner, j).start())

        loop(1, groups, one)

    def gather_finish(a):
        def one(j):
            peer = near(j)
            wait_block(a, peer)
            loop(1, groups, lambda k: wait_block(
                a, lax.rem(hi + groups - k, groups) * group + lax.rem(lo + j, group)))

        loop(1, group, one)
        own_copy(a).wait()

    def gather_drain(a):
        loop(1, groups, lambda k: own_send(a, far(k)).wait_send())
        loop(1, group, lambda j: own_send(a, near(j)).wait_send())
        loop(1, groups, lambda k: loop(
            1, group, lambda j: forward_send(a, far_from(k), j).wait_send()))

    def core_copy(m, c):
        return pltpu.make_async_remote_copy(
            src_ref=part.at[m, c, theirs, :],
            dst_ref=core_in.at[m, c],
            send_sem=core_send_sem.at[m, c],
            recv_sem=core_recv_sem.at[m, c],
            device_id={"row": core_peer},
            device_id_type=MESH,
        )

    def x_copy(m, c):
        return pltpu.make_async_remote_copy(
            src_ref=x_send.at[m, c],
            dst_ref=x_in.at[m, c],
            send_sem=x_send_sem.at[m, c],
            recv_sem=x_recv_sem.at[m, c],
            device_id={"row": x_peer},
            device_id_type=MESH,
        )

    def res_copy(c):
        return pltpu.make_async_remote_copy(
            src_ref=res.at[c, :, mine, :],
            dst_ref=res.at[c, :, mine, :],
            send_sem=res_send_sem.at[c],
            recv_sem=res_recv_sem.at[c],
            device_id={"row": core_peer},
            device_id_type=MESH,
        )

    def out_copy(k, c):
        target = (hid_out, dgate_out, dup_out)[k]
        return pltpu.make_async_copy(res.at[c, k], target.at[:, columns(c)], out_sem.at[k, c])

    def multiply(m, c):
        weight_copy(m, c).wait()
        if m == 2:
            part[m, c] = contract_last(grad[...], wd[columns(c), :])
        else:
            weight = (wg, wu)[m]
            part[m, c] = jnp.dot(tok[...], weight[:, columns(c)], preferred_element_type=F32)
        core_copy(m, c).start()

    def chip_sum(m, c):
        core_copy(m, c).wait_recv()
        value = part[m, c, mine, :] + core_in[m, c]
        part[m, c, mine, :] = value
        x_send[m, c] = value.astype(BF16)
        x_copy(m, c).start()

    def gate_up(c):
        multiply(0, c)
        multiply(1, c)

        @pl.when(c > 0)
        def _():
            chip_sum(0, c - 1)
            chip_sum(1, c - 1)

    def down(c):
        multiply(2, c)

        @pl.when(c == 0)
        def _():
            chip_sum(0, chunks - 1)
            chip_sum(1, chunks - 1)

        @pl.when(c > 0)
        def _():
            chip_sum(2, c - 1)

    def input_product(c):
        res_copy(c).wait_recv()
        for k in range(3):
            out_copy(k, c).start()
        acc[...] += contract_last(res[c, 1], wg[:, columns(c)])
        acc[...] += contract_last(res[c, 2], wu[:, columns(c)])

    def finish(c):
        for m in range(3):
            x_copy(m, c).wait_recv()
        values = [part[m, c, mine, :] + x_in[m, c].astype(F32) for m in range(3)]
        for k, value in enumerate(pointwise(*values)):
            res[c, k, mine, :] = value
        res_copy(c).start()

        @pl.when(c > 0)
        def _():
            input_product(c - 1)

    loop(0, chunks, load_pair)
    loop(0, chunks, lambda c: weight_copy(2, c).start())
    acc[...] = jnp.zeros_like(acc)

    barrier = pltpu.get_barrier_semaphore()
    loop(1, groups, lambda k: pl.semaphore_signal(
        barrier, inc=1, device_id={"col": far(k)}, device_id_type=MESH))
    loop(1, group, lambda j: pl.semaphore_signal(
        barrier, inc=1, device_id={"col": near(j)}, device_id_type=MESH))
    for peer in (core_peer, x_peer):
        pl.semaphore_signal(barrier, inc=1, device_id={"row": peer}, device_id_type=MESH)
    pl.semaphore_wait(barrier, groups + group)

    gather_start(0)
    gather_forward(0)
    gather_start(1)
    gather_finish(0)
    early = min(3, chunks)
    loop(0, early, gate_up)
    gather_forward(1)
    loop(early, chunks, gate_up)
    gather_finish(1)
    tok_copy = pltpu.make_async_copy(tok, tok_out, full_sem.at[0])
    grad_copy = pltpu.make_async_copy(grad, grad_out, full_sem.at[1])
    tok_copy.start()
    grad_copy.start()
    loop(0, chunks, down)
    chip_sum(2, chunks - 1)
    loop(0, chunks, finish)
    input_product(chunks - 1)

    for k in range(n):
        owner = lax.rem(me + k, n)
        partial_outs[k][...] = acc[place(owner), :].astype(BF16)

    gather_drain(0)
    gather_drain(1)

    def drain(c):
        for m in range(3):
            core_copy(m, c).wait_send()
            x_copy(m, c).wait_send()
            out_copy(m, c).wait()
        res_copy(c).wait_send()

    loop(0, chunks, drain)
    tok_copy.wait()
    grad_copy.wait()


def forward(n, tokens, out_grad, gate_w, up_w, down_w):
    block, depth = tokens.shape
    units = gate_w.shape[1]
    total = block * n
    width = chunk_width(units)
    chunks = units // width
    group = 2 if n % 2 == 0 else 1
    half = total // 2
    anywhere = pl.BlockSpec(memory_space=pl.ANY)
    inside = pl.BlockSpec(memory_space=pltpu.VMEM)
    full = jax.ShapeDtypeStruct((total, depth), BF16)
    hidden = jax.ShapeDtypeStruct((total, units), BF16)
    piece = jax.ShapeDtypeStruct((block, depth), BF16)
    dma = pltpu.SemaphoreType.DMA
    return pl.pallas_call(
        functools.partial(forward_kernel, n, group, chunks, width),
        out_shape=[full] * 2 + [hidden] * 3 + [piece] * n,
        in_specs=[anywhere] * 5,
        out_specs=[anywhere] * 5 + [inside] * n,
        scratch_shapes=[
            pltpu.VMEM((total, depth), BF16),
            pltpu.VMEM((total, depth), BF16),
            pltpu.VMEM((depth, units), BF16),
            pltpu.VMEM((depth, units), BF16),
            pltpu.VMEM((units, depth), BF16),
            pltpu.VMEM((3, chunks, total, width), F32),
            pltpu.VMEM((3, chunks, half, width), F32),
            pltpu.VMEM((3, chunks, half, width), BF16),
            pltpu.VMEM((3, chunks, half, width), BF16),
            pltpu.VMEM((chunks, 3, total, width), BF16),
            pltpu.VMEM((total, depth), F32),
            dma((3, chunks)),
            dma((2,)),
            dma((2, n)),
            dma((2, n, group)),
            dma((2, n)),
            dma((3, chunks)),
            dma((3, chunks)),
            dma((3, chunks)),
            dma((3, chunks)),
            dma((chunks,)),
            dma((chunks,)),
            dma((3, chunks)),
            dma((2,)),
        ],
        compiler_params=pltpu.CompilerParams(
            collective_id=0, has_side_effects=True, vmem_limit_bytes=63 * 2**20
        ),
        name="forward_exchange",
    )(tokens, out_grad, gate_w, up_w, down_w)


def grads_kernel(tok, grad, hidden, d_gate, d_up, gate_o, up_o, down_o, tok_t, hid_t):
    step = pl.program_id(0)

    @pl.when(step == 0)
    def _():
        tok_t[...] = tok[...].T
        hid_t[...] = hidden[...].T

    rows = gate_o.shape[0]
    left = tok_t[pl.ds(pl.multiple_of(step * rows, rows), rows), :]
    gate_o[...] = jnp.dot(left, d_gate[...], preferred_element_type=F32).astype(BF16)
    up_o[...] = jnp.dot(left, d_up[...], preferred_element_type=F32).astype(BF16)
    units = down_o.shape[0]
    left = hid_t[pl.ds(pl.multiple_of(step * units, units), units), :]
    down_o[...] = jnp.dot(left, grad[...], preferred_element_type=F32).astype(BF16)


def weight_grads(tok, grad, hidden, d_gate, d_up):
    total, depth = tok.shape
    units = hidden.shape[1]
    steps = max(s for s in (1, 2, 4, 8) if depth % (16 * s) == 0 and units % (16 * s) == 0)
    inside = pl.BlockSpec(memory_space=pltpu.VMEM)
    wide = pl.BlockSpec((depth // steps, units), lambda i: (i, 0))
    tall = pl.BlockSpec((units // steps, depth), lambda i: (i, 0))
    return pl.pallas_call(
        grads_kernel,
        grid=(steps,),
        out_shape=[
            jax.ShapeDtypeStruct((depth, units), BF16),
            jax.ShapeDtypeStruct((depth, units), BF16),
            jax.ShapeDtypeStruct((units, depth), BF16),
        ],
        in_specs=[inside] * 5,
        out_specs=[wide, wide, tall],
        scratch_shapes=[pltpu.VMEM((depth, total), BF16), pltpu.VMEM((units, total), BF16)],
        compiler_params=pltpu.CompilerParams(vmem_limit_bytes=48 * 2**20),
        cost_estimate=pl.CostEstimate(
            flops=6 * total * depth * units, bytes_accessed=6 * depth * units, transcendentals=0
        ),
        name="weight_grads",
    )(tok, grad, hidden, d_gate, d_up)


def local(n, tokens, out_grad, gate_weight, up_weight, down_weight):
    tok, grad, hidden, d_gate, d_up, *pieces = forward(
        n, tokens, out_grad, gate_weight, up_weight, down_weight
    )
    arrived = [
        lax.ppermute(pieces[k], "col", [(i, (i + k) % n) for i in range(n)]) for k in range(1, n)
    ]
    grad_gate, grad_up, grad_down = weight_grads(tok, grad, hidden, d_gate, d_up)
    total = pieces[0].astype(F32)
    for piece in arrived:
        total = total + piece.astype(F32)
    return total.astype(BF16), grad_gate, grad_up, grad_down


def solution(mesh):
    in_specs = (P("col", "row"), P("col", "row"), P("row", "col"), P("row", "col"), P("col", "row"))
    out_specs = (P("col", "row"), P("row", "col"), P("row", "col"), P("col", "row"))
    return jax.shard_map(
        functools.partial(local, mesh.shape["col"]),
        mesh=mesh, in_specs=in_specs, out_specs=out_specs, check_vma=False,
    )
```

```python
import functools

import jax
import jax.numpy as jnp
from jax import lax
from jax.experimental import pallas as pl
from jax.experimental.pallas import tpu as pltpu
from jax.sharding import PartitionSpec as P

MESH = pl.DeviceIdType.MESH
F32, BF16 = jnp.float32, jnp.bfloat16


def pointwise(gate, up, hidden_grad):
    logistic = jax.nn.sigmoid(gate)
    active = gate * logistic
    hidden = (active * up).astype(BF16)
    d_gate = (hidden_grad * up * logistic * (1.0 + gate * (1.0 - logistic))).astype(BF16)
    d_up = (hidden_grad * active).astype(BF16)
    return hidden, d_gate, d_up


def chunk_width(units):
    for width in (512, 256, 128):
        if units % width == 0:
            return width
    return units


def loop(low, high, body):
    def step(index, carry):
        body(index)
        return carry

    lax.fori_loop(low, high, step, 0)


def forward_kernel(
    n, group, chunks, width,
    tokens, out_grad, gate_w, up_w, down_w,
    tok_out, grad_out, hid_out, dgate_out, dup_out, keep_out, send_out,
    *scratch,
):
    (
        tok, grad, tok_t, grad_t, hid_t, wg, wu, wd, part, core_in, x_send, x_in, res, turned, acc_t, acc,
        w_sem, own_sem, ag_send, ag_fwd, ag_recv,
        core_send_sem, core_recv_sem, x_send_sem, x_recv_sem, res_send_sem, res_recv_sem,
        out_sem, full_sem,
    ) = scratch
    block = tokens.shape[0]
    bands = 512 if tokens.shape[1] % 512 == 0 else tokens.shape[1]
    total = block * n
    half = total // 2
    row, me = lax.axis_index("row"), lax.axis_index("col")
    core = lax.rem(row, 2)
    core_peer = row + 1 - 2 * core
    x_peer = lax.rem(row + 2, 4)
    groups = n // group
    hi, lo = me // group, lax.rem(me, group)
    mine = pl.ds(pl.multiple_of(core * half, half), half)
    theirs = pl.ds(pl.multiple_of((1 - core) * half, half), half)

    def columns(c):
        return pl.ds(pl.multiple_of(c * width, width), width)

    def weight_copy(m, c):
        if m == 2:
            return pltpu.make_async_copy(
                down_w.at[columns(c), :], wd.at[columns(c), :], w_sem.at[m, c]
            )
        source, target = ((gate_w, wg), (up_w, wu))[m]
        return pltpu.make_async_copy(
            source.at[:, columns(c)], target.at[:, columns(c)], w_sem.at[m, c]
        )

    def load_pair(c):
        weight_copy(0, c).start()
        weight_copy(1, c).start()

    def place(owner):
        return pl.ds(pl.multiple_of(owner * block, block), block)

    def far(k):
        return lax.rem(hi + k, groups) * group + lo

    def far_from(k):
        return lax.rem(hi + groups - k, groups) * group + lo

    def near(j):
        return hi * group + lax.rem(lo + j, group)

    arrays = ((tokens, tok), (out_grad, grad))

    def own_copy(a):
        return pltpu.make_async_copy(arrays[a][0], arrays[a][1].at[place(me), :], own_sem.at[a])

    def own_send(a, peer):
        return pltpu.make_async_remote_copy(
            src_ref=arrays[a][0],
            dst_ref=arrays[a][1].at[place(me), :],
            send_sem=ag_send.at[a, peer],
            recv_sem=ag_recv.at[a, me],
            device_id={"col": peer},
            device_id_type=MESH,
        )

    def forward_send(a, owner, j):
        return pltpu.make_async_remote_copy(
            src_ref=arrays[a][1].at[place(owner), :],
            dst_ref=arrays[a][1].at[place(owner), :],
            send_sem=ag_fwd.at[a, owner, j],
            recv_sem=ag_recv.at[a, owner],
            device_id={"col": near(j)},
            device_id_type=MESH,
        )

    def wait_block(a, owner):
        pltpu.make_async_copy(
            arrays[a][0], arrays[a][1].at[place(owner), :], ag_recv.at[a, owner]
        ).wait()

    def gather_start(a):
        own_copy(a).start()
        loop(1, groups, lambda k: own_send(a, far(k)).start())
        loop(1, group, lambda j: own_send(a, near(j)).start())

    def gather_forward(a):
        def one(k):
            owner = far_from(k)
            wait_block(a, owner)
            loop(1, group, lambda j: forward_send(a, owner, j).start())

        loop(1, groups, one)

    def gather_finish(a):
        def one(j):
            peer = near(j)
            wait_block(a, peer)
            loop(1, groups, lambda k: wait_block(
                a, lax.rem(hi + groups - k, groups) * group + lax.rem(lo + j, group)))

        loop(1, group, one)
        own_copy(a).wait()

    def gather_drain(a):
        loop(1, groups, lambda k: own_send(a, far(k)).wait_send())
        loop(1, group, lambda j: own_send(a, near(j)).wait_send())
        loop(1, groups, lambda k: loop(
            1, group, lambda j: forward_send(a, far_from(k), j).wait_send()))

    def core_copy(m, c):
        return pltpu.make_async_remote_copy(
            src_ref=part.at[m, c, theirs, :],
            dst_ref=core_in.at[m, c],
            send_sem=core_send_sem.at[m, c],
            recv_sem=core_recv_sem.at[m, c],
            device_id={"row": core_peer},
            device_id_type=MESH,
        )

    def x_copy(m, c):
        return pltpu.make_async_remote_copy(
            src_ref=x_send.at[m, c],
            dst_ref=x_in.at[m, c],
            send_sem=x_send_sem.at[m, c],
            recv_sem=x_recv_sem.at[m, c],
            device_id={"row": x_peer},
            device_id_type=MESH,
        )

    def res_copy(c):
        return pltpu.make_async_remote_copy(
            src_ref=res.at[c, :, mine, :],
            dst_ref=res.at[c, :, mine, :],
            send_sem=res_send_sem.at[c],
            recv_sem=res_recv_sem.at[c],
            device_id={"row": core_peer},
            device_id_type=MESH,
        )

    def out_copy(k, c):
        if k == 0:
            return pltpu.make_async_copy(
                hid_t.at[columns(c), :], hid_out.at[columns(c), :], out_sem.at[k, c]
            )
        target = (dgate_out, dup_out)[k - 1]
        return pltpu.make_async_copy(res.at[c, k], target.at[:, columns(c)], out_sem.at[k, c])

    def multiply(m, c):
        weight_copy(m, c).wait()
        if m == 2:
            part[m, c] = jnp.dot(
                wd[columns(c), :], grad_t[...], preferred_element_type=F32
            ).T
        else:
            weight = (wg, wu)[m]
            part[m, c] = jnp.dot(tok[...], weight[:, columns(c)], preferred_element_type=F32)
        core_copy(m, c).start()

    def chip_sum(m, c):
        core_copy(m, c).wait_recv()
        value = part[m, c, mine, :] + core_in[m, c]
        part[m, c, mine, :] = value
        x_send[m, c] = value.astype(BF16)
        x_copy(m, c).start()

    def gate_up(c):
        multiply(0, c)
        multiply(1, c)

        @pl.when(c > 0)
        def _():
            chip_sum(0, c - 1)
            chip_sum(1, c - 1)

    def down(c):
        multiply(2, c)

        @pl.when(c == 0)
        def _():
            chip_sum(0, chunks - 1)
            chip_sum(1, chunks - 1)

        @pl.when(c > 0)
        def _():
            chip_sum(2, c - 1)

    def input_product(c):
        res_copy(c).wait_recv()
        out_copy(1, c).start()
        out_copy(2, c).start()
        hid_t[columns(c), :] = res[c, 0].T
        out_copy(0, c).start()
        turned[0] = res[c, 1].T
        turned[1] = res[c, 2].T

        def band(r):
            rows = pl.ds(pl.multiple_of(r * bands, bands), bands)
            acc_t[rows, :] += jnp.dot(
                wg[rows, columns(c)], turned[0], preferred_element_type=F32
            ) + jnp.dot(wu[rows, columns(c)], turned[1], preferred_element_type=F32)

        loop(0, acc_t.shape[0] // bands, band)

    def finish(c):
        for m in range(3):
            x_copy(m, c).wait_recv()
        values = [part[m, c, mine, :] + x_in[m, c].astype(F32) for m in range(3)]
        for k, value in enumerate(pointwise(*values)):
            res[c, k, mine, :] = value
        res_copy(c).start()

        @pl.when(c > 0)
        def _():
            input_product(c - 1)

    loop(0, chunks, load_pair)
    loop(0, chunks, lambda c: weight_copy(2, c).start())
    acc_t[...] = jnp.zeros_like(acc_t)

    barrier = pltpu.get_barrier_semaphore()
    loop(1, groups, lambda k: pl.semaphore_signal(
        barrier, inc=1, device_id={"col": far(k)}, device_id_type=MESH))
    loop(1, group, lambda j: pl.semaphore_signal(
        barrier, inc=1, device_id={"col": near(j)}, device_id_type=MESH))
    for peer in (core_peer, x_peer):
        pl.semaphore_signal(barrier, inc=1, device_id={"row": peer}, device_id_type=MESH)
    pl.semaphore_wait(barrier, groups + group)

    gather_start(0)
    gather_forward(0)
    gather_start(1)
    gather_finish(0)
    early = min(3, chunks)
    loop(0, early, gate_up)
    gather_forward(1)
    loop(early, chunks, gate_up)
    gather_finish(1)
    grad_copy = pltpu.make_async_copy(grad, grad_out, full_sem.at[1])
    grad_copy.start()
    grad_t[...] = grad[...].T
    loop(0, chunks, down)
    tok_t[...] = tok[...].T
    tok_copy = pltpu.make_async_copy(tok_t, tok_out, full_sem.at[0])
    tok_copy.start()
    chip_sum(2, chunks - 1)
    loop(0, chunks, finish)
    input_product(chunks - 1)

    acc[...] = acc_t[...].T
    side = lax.rem(me, 2)
    for k in range(n // 2):
        keep_out[k] = acc[place(2 * k + side), :]
        send_out[k] = acc[place(2 * k + 1 - side), :].astype(BF16)

    gather_drain(0)
    gather_drain(1)

    def drain(c):
        for m in range(3):
            core_copy(m, c).wait_send()
            x_copy(m, c).wait_send()
            out_copy(m, c).wait()
        res_copy(c).wait_send()

    loop(0, chunks, drain)
    tok_copy.wait()
    grad_copy.wait()


def forward(n, tokens, out_grad, gate_w, up_w, down_w):
    block, depth = tokens.shape
    units = gate_w.shape[1]
    total = block * n
    width = chunk_width(units)
    chunks = units // width
    group = 2
    half = total // 2
    anywhere = pl.BlockSpec(memory_space=pl.ANY)
    inside = pl.BlockSpec(memory_space=pltpu.VMEM)
    full = jax.ShapeDtypeStruct((total, depth), BF16)
    hidden = jax.ShapeDtypeStruct((total, units), BF16)
    turned = jax.ShapeDtypeStruct((depth, total), BF16)
    hidden_t = jax.ShapeDtypeStruct((units, total), BF16)
    dma = pltpu.SemaphoreType.DMA
    return pl.pallas_call(
        functools.partial(forward_kernel, n, group, chunks, width),
        out_shape=[
            turned, full, hidden_t, hidden, hidden,
            jax.ShapeDtypeStruct((n // 2, block, depth), F32),
            jax.ShapeDtypeStruct((n // 2, block, depth), BF16),
        ],
        in_specs=[anywhere] * 5,
        out_specs=[anywhere] * 5 + [inside] * 2,
        scratch_shapes=[
            pltpu.VMEM((total, depth), BF16),
            pltpu.VMEM((total, depth), BF16),
            pltpu.VMEM((depth, total), BF16),
            pltpu.VMEM((depth, total), BF16),
            pltpu.VMEM((units, total), BF16),
            pltpu.VMEM((depth, units), BF16),
            pltpu.VMEM((depth, units), BF16),
            pltpu.VMEM((units, depth), BF16),
            pltpu.VMEM((3, chunks, total, width), F32),
            pltpu.VMEM((3, chunks, half, width), F32),
            pltpu.VMEM((3, chunks, half, width), BF16),
            pltpu.VMEM((3, chunks, half, width), BF16),
            pltpu.VMEM((chunks, 3, total, width), BF16),
            pltpu.VMEM((2, width, total), BF16),
            pltpu.VMEM((depth, total), F32),
            pltpu.VMEM((total, depth), F32),
            dma((3, chunks)),
            dma((2,)),
            dma((2, n)),
            dma((2, n, group)),
            dma((2, n)),
            dma((3, chunks)),
            dma((3, chunks)),
            dma((3, chunks)),
            dma((3, chunks)),
            dma((chunks,)),
            dma((chunks,)),
            dma((3, chunks)),
            dma((2,)),
        ],
        compiler_params=pltpu.CompilerParams(
            collective_id=0, has_side_effects=True, vmem_limit_bytes=63 * 2**20
        ),
        name="forward_exchange",
    )(tokens, out_grad, gate_w, up_w, down_w)


def grad_kernel(left, right, out):
    out[...] = jnp.dot(left[...], right[...], preferred_element_type=F32).astype(BF16)


def weight_grad(name, grant, left, right):
    rows, total = left.shape
    width = right.shape[1]
    steps = max(s for s in (1, 2, 4, 8) if rows % (16 * s) == 0)
    return pl.pallas_call(
        grad_kernel,
        grid=(steps,),
        out_shape=jax.ShapeDtypeStruct((rows, width), BF16),
        in_specs=[
            pl.BlockSpec((rows // steps, total), lambda i: (i, 0)),
            pl.BlockSpec((total, width), lambda i: (0, 0)),
        ],
        out_specs=pl.BlockSpec((rows // steps, width), lambda i: (i, 0)),
        compiler_params=pltpu.CompilerParams(vmem_limit_bytes=grant * 2**20),
        cost_estimate=pl.CostEstimate(
            flops=2 * total * rows * width, bytes_accessed=2 * rows * width, transcendentals=0
        ),
        name=name,
    )(left, right)


def local(n, tokens, out_grad, gate_weight, up_weight, down_weight):
    tok_t, grad, hid_t, d_gate, d_up, keep, send = forward(
        n, tokens, out_grad, gate_weight, up_weight, down_weight
    )
    products = [("grad_gate", tok_t, d_gate), ("grad_up", tok_t, d_up), ("grad_down", hid_t, grad)]
    results = []
    me = lax.axis_index("col")
    bit, left = 1, n // 2
    while True:
        arrived = lax.ppermute(send, "col", [(i, i ^ bit) for i in range(n)])
        if products:
            name, first, second = products.pop(0)
            if results:
                second, _ = lax.optimization_barrier((second, send))
            results.append(weight_grad(name, 48 if results else 62, first, second))
        bit *= 2
        if left == 1:
            break
        left //= 2
        pair = (left, 2) + keep.shape[1:]
        side = (me // bit) % 2
        halves = [
            lax.dynamic_index_in_dim(keep.reshape(pair), s, 1, False)
            + lax.dynamic_index_in_dim(arrived.reshape(pair), s, 1, False).astype(F32)
            for s in (side, 1 - side)
        ]
        keep, send = halves[0], halves[1].astype(BF16)
    for name, first, second in products:
        results.append(weight_grad(name, 48, first, second))
    total = keep[0] + arrived[0].astype(F32)
    return (total.astype(BF16), *results)


def solution(mesh):
    in_specs = (P("col", "row"), P("col", "row"), P("row", "col"), P("row", "col"), P("col", "row"))
    out_specs = (P("col", "row"), P("row", "col"), P("row", "col"), P("col", "row"))
    return jax.shard_map(
        functools.partial(local, mesh.shape["col"]),
        mesh=mesh, in_specs=in_specs, out_specs=out_specs, check_vma=False,
    )
```

```python
import functools

import jax
import jax.numpy as jnp
from jax import lax
from jax.experimental import pallas as pl
from jax.experimental.pallas import tpu as pltpu
from jax.sharding import PartitionSpec as P

MESH = pl.DeviceIdType.MESH
F32, BF16 = jnp.float32, jnp.bfloat16


def pointwise(gate, up, hidden_grad):
    logistic = jax.nn.sigmoid(gate)
    active = gate * logistic
    hidden = (active * up).astype(BF16)
    d_gate = (hidden_grad * up * logistic * (1.0 + gate * (1.0 - logistic))).astype(BF16)
    d_up = (hidden_grad * active).astype(BF16)
    return hidden, d_gate, d_up


def contract_last(left, right):
    return lax.dot_general(left, right, (((1,), (1,)), ((), ())), preferred_element_type=F32)


def chunk_width(units):
    for width in (512, 256, 128):
        if units % width == 0:
            return width
    return units


def loop(low, high, body):
    def step(index, carry):
        body(index)
        return carry

    lax.fori_loop(low, high, step, 0)


def forward_kernel(
    n, group, chunks, width,
    tokens, out_grad, gate_w, up_w, down_w,
    tok_out, grad_out, hid_out, dgate_out, dup_out, pieces_out,
    *scratch,
):
    (
        tok, grad, tok_t, hid_t, wg, wu, wd, part, core_in, x_send, x_in, res, acc,
        w_sem, own_sem, ag_send, ag_fwd, ag_recv,
        core_send_sem, core_recv_sem, x_send_sem, x_recv_sem, res_send_sem, res_recv_sem,
        out_sem, full_sem,
    ) = scratch
    block = tokens.shape[0]
    total = block * n
    half = total // 2
    row, me = lax.axis_index("row"), lax.axis_index("col")
    core = lax.rem(row, 2)
    core_peer = row + 1 - 2 * core
    x_peer = lax.rem(row + 2, 4)
    groups = n // group
    hi, lo = me // group, lax.rem(me, group)
    mine = pl.ds(pl.multiple_of(core * half, half), half)
    theirs = pl.ds(pl.multiple_of((1 - core) * half, half), half)

    def columns(c):
        return pl.ds(pl.multiple_of(c * width, width), width)

    def weight_copy(m, c):
        if m == 2:
            return pltpu.make_async_copy(
                down_w.at[columns(c), :], wd.at[columns(c), :], w_sem.at[m, c]
            )
        source, target = ((gate_w, wg), (up_w, wu))[m]
        return pltpu.make_async_copy(
            source.at[:, columns(c)], target.at[:, columns(c)], w_sem.at[m, c]
        )

    def load_pair(c):
        weight_copy(0, c).start()
        weight_copy(1, c).start()

    def place(owner):
        return pl.ds(pl.multiple_of(owner * block, block), block)

    def far(k):
        return lax.rem(hi + k, groups) * group + lo

    def far_from(k):
        return lax.rem(hi + groups - k, groups) * group + lo

    def near(j):
        return hi * group + lax.rem(lo + j, group)

    arrays = ((tokens, tok), (out_grad, grad))

    def own_copy(a):
        return pltpu.make_async_copy(arrays[a][0], arrays[a][1].at[place(me), :], own_sem.at[a])

    def own_send(a, peer):
        return pltpu.make_async_remote_copy(
            src_ref=arrays[a][0],
            dst_ref=arrays[a][1].at[place(me), :],
            send_sem=ag_send.at[a, peer],
            recv_sem=ag_recv.at[a, me],
            device_id={"col": peer},
            device_id_type=MESH,
        )

    def forward_send(a, owner, j):
        return pltpu.make_async_remote_copy(
            src_ref=arrays[a][1].at[place(owner), :],
            dst_ref=arrays[a][1].at[place(owner), :],
            send_sem=ag_fwd.at[a, owner, j],
            recv_sem=ag_recv.at[a, owner],
            device_id={"col": near(j)},
            device_id_type=MESH,
        )

    def wait_block(a, owner):
        pltpu.make_async_copy(
            arrays[a][0], arrays[a][1].at[place(owner), :], ag_recv.at[a, owner]
        ).wait()

    def gather_start(a):
        own_copy(a).start()
        loop(1, groups, lambda k: own_send(a, far(k)).start())
        loop(1, group, lambda j: own_send(a, near(j)).start())

    def gather_forward(a):
        def one(k):
            owner = far_from(k)
            wait_block(a, owner)
            loop(1, group, lambda j: forward_send(a, owner, j).start())

        loop(1, groups, one)

    def gather_finish(a):
        def one(j):
            peer = near(j)
            wait_block(a, peer)
            loop(1, groups, lambda k: wait_block(
                a, lax.rem(hi + groups - k, groups) * group + lax.rem(lo + j, group)))

        loop(1, group, one)
        own_copy(a).wait()

    def gather_drain(a):
        loop(1, groups, lambda k: own_send(a, far(k)).wait_send())
        loop(1, group, lambda j: own_send(a, near(j)).wait_send())
        loop(1, groups, lambda k: loop(
            1, group, lambda j: forward_send(a, far_from(k), j).wait_send()))

    def core_copy(m, c):
        return pltpu.make_async_remote_copy(
            src_ref=part.at[m, c, theirs, :],
            dst_ref=core_in.at[m, c],
            send_sem=core_send_sem.at[m, c],
            recv_sem=core_recv_sem.at[m, c],
            device_id={"row": core_peer},
            device_id_type=MESH,
        )

    def x_copy(m, c):
        return pltpu.make_async_remote_copy(
            src_ref=x_send.at[m, c],
            dst_ref=x_in.at[m, c],
            send_sem=x_send_sem.at[m, c],
            recv_sem=x_recv_sem.at[m, c],
            device_id={"row": x_peer},
            device_id_type=MESH,
        )

    def res_copy(c):
        return pltpu.make_async_remote_copy(
            src_ref=res.at[c, :, mine, :],
            dst_ref=res.at[c, :, mine, :],
            send_sem=res_send_sem.at[c],
            recv_sem=res_recv_sem.at[c],
            device_id={"row": core_peer},
            device_id_type=MESH,
        )

    def out_copy(k, c):
        if k == 0:
            return pltpu.make_async_copy(
                hid_t.at[columns(c), :], hid_out.at[columns(c), :], out_sem.at[k, c]
            )
        target = (dgate_out, dup_out)[k - 1]
        return pltpu.make_async_copy(res.at[c, k], target.at[:, columns(c)], out_sem.at[k, c])

    def multiply(m, c):
        weight_copy(m, c).wait()
        if m == 2:
            part[m, c] = contract_last(grad[...], wd[columns(c), :])
        else:
            weight = (wg, wu)[m]
            part[m, c] = jnp.dot(tok[...], weight[:, columns(c)], preferred_element_type=F32)
        core_copy(m, c).start()

    def chip_sum(m, c):
        core_copy(m, c).wait_recv()
        value = part[m, c, mine, :] + core_in[m, c]
        part[m, c, mine, :] = value
        x_send[m, c] = value.astype(BF16)
        x_copy(m, c).start()

    def gate_up(c):
        multiply(0, c)

        @pl.when(c > 0)
        def _():
            chip_sum(1, c - 1)

        multiply(1, c)
        chip_sum(0, c)

    def down(c):
        multiply(2, c)

        @pl.when(c > 0)
        def _():
            chip_sum(2, c - 1)

    def later(c):
        multiply(0, c)
        multiply(1, c)
        chip_sum(0, c)
        multiply(2, c)
        chip_sum(1, c)
        finish(c - early)
        chip_sum(2, c)

    def input_product(c):
        res_copy(c).wait_recv()
        out_copy(1, c).start()
        out_copy(2, c).start()
        hid_t[columns(c), :] = res[c, 0].T
        out_copy(0, c).start()
        acc[...] += contract_last(res[c, 1], wg[:, columns(c)])
        acc[...] += contract_last(res[c, 2], wu[:, columns(c)])

    def finish(c):
        for m in range(3):
            x_copy(m, c).wait_recv()
        values = [part[m, c, mine, :] + x_in[m, c].astype(F32) for m in range(3)]
        for k, value in enumerate(pointwise(*values)):
            res[c, k, mine, :] = value
        res_copy(c).start()

        @pl.when(c > 0)
        def _():
            input_product(c - 1)

    loop(0, chunks, load_pair)
    loop(0, chunks, lambda c: weight_copy(2, c).start())
    acc[...] = jnp.zeros_like(acc)

    barrier = pltpu.get_barrier_semaphore()
    loop(1, groups, lambda k: pl.semaphore_signal(
        barrier, inc=1, device_id={"col": far(k)}, device_id_type=MESH))
    loop(1, group, lambda j: pl.semaphore_signal(
        barrier, inc=1, device_id={"col": near(j)}, device_id_type=MESH))
    for peer in (core_peer, x_peer):
        pl.semaphore_signal(barrier, inc=1, device_id={"row": peer}, device_id_type=MESH)
    pl.semaphore_wait(barrier, groups + group)

    gather_start(0)
    gather_forward(0)
    gather_start(1)
    gather_finish(0)
    early = min(3, chunks)
    loop(0, early, gate_up)
    chip_sum(1, early - 1)
    gather_forward(1)
    tok_t[...] = tok[...].T
    tok_copy = pltpu.make_async_copy(tok_t, tok_out, full_sem.at[0])
    tok_copy.start()
    gather_finish(1)
    grad_copy = pltpu.make_async_copy(grad, grad_out, full_sem.at[1])
    grad_copy.start()
    loop(0, early, down)
    chip_sum(2, early - 1)
    loop(early, chunks, later)
    loop(chunks - early, chunks, finish)
    input_product(chunks - 1)

    for k in range(n):
        pieces_out[k] = acc[k * block : (k + 1) * block, :].astype(BF16)

    gather_drain(0)
    gather_drain(1)

    def drain(c):
        for m in range(3):
            core_copy(m, c).wait_send()
            x_copy(m, c).wait_send()
            out_copy(m, c).wait()
        res_copy(c).wait_send()

    loop(0, chunks, drain)
    tok_copy.wait()
    grad_copy.wait()


def forward(n, tokens, out_grad, gate_w, up_w, down_w):
    block, depth = tokens.shape
    units = gate_w.shape[1]
    total = block * n
    width = chunk_width(units)
    chunks = units // width
    group = 2
    half = total // 2
    anywhere = pl.BlockSpec(memory_space=pl.ANY)
    inside = pl.BlockSpec(memory_space=pltpu.VMEM)
    full = jax.ShapeDtypeStruct((total, depth), BF16)
    hidden = jax.ShapeDtypeStruct((total, units), BF16)
    turned = jax.ShapeDtypeStruct((depth, total), BF16)
    hidden_t = jax.ShapeDtypeStruct((units, total), BF16)
    dma = pltpu.SemaphoreType.DMA
    return pl.pallas_call(
        functools.partial(forward_kernel, n, group, chunks, width),
        out_shape=[
            turned, full, hidden_t, hidden, hidden,
            jax.ShapeDtypeStruct((n, block, depth), BF16),
        ],
        in_specs=[anywhere] * 5,
        out_specs=[anywhere] * 5 + [inside],
        scratch_shapes=[
            pltpu.VMEM((total, depth), BF16),
            pltpu.VMEM((total, depth), BF16),
            pltpu.VMEM((depth, total), BF16),
            pltpu.VMEM((units, total), BF16),
            pltpu.VMEM((depth, units), BF16),
            pltpu.VMEM((depth, units), BF16),
            pltpu.VMEM((units, depth), BF16),
            pltpu.VMEM((3, chunks, total, width), F32),
            pltpu.VMEM((3, chunks, half, width), F32),
            pltpu.VMEM((3, chunks, half, width), BF16),
            pltpu.VMEM((3, chunks, half, width), BF16),
            pltpu.VMEM((chunks, 3, total, width), BF16),
            pltpu.VMEM((total, depth), F32),
            dma((3, chunks)),
            dma((2,)),
            dma((2, n)),
            dma((2, n, group)),
            dma((2, n)),
            dma((3, chunks)),
            dma((3, chunks)),
            dma((3, chunks)),
            dma((3, chunks)),
            dma((chunks,)),
            dma((chunks,)),
            dma((3, chunks)),
            dma((2,)),
        ],
        compiler_params=pltpu.CompilerParams(
            collective_id=0, has_side_effects=True, vmem_limit_bytes=63 * 2**20
        ),
        name="forward_exchange",
    )(tokens, out_grad, gate_w, up_w, down_w)


def grads_kernel(tok_t, hid_t, d_gate, d_up, grad, gate_o, up_o, down_o):
    for left, right, out in (
        (tok_t, d_gate, gate_o), (tok_t, d_up, up_o), (hid_t, grad, down_o)
    ):
        out[...] = jnp.dot(left[...], right[...], preferred_element_type=F32).astype(BF16)


def weight_grads(tok_t, hid_t, d_gate, d_up, grad):
    depth, total = tok_t.shape
    units = hid_t.shape[0]
    steps = max(s for s in (1, 2, 4, 8) if depth % (16 * s) == 0 and units % (16 * s) == 0)

    def rows(count, width):
        return pl.BlockSpec((count // steps, width), lambda i: (i, 0))

    def whole(array):
        return pl.BlockSpec(array.shape, lambda i: (0, 0))

    return pl.pallas_call(
        grads_kernel,
        grid=(steps,),
        out_shape=[
            jax.ShapeDtypeStruct((depth, units), BF16),
            jax.ShapeDtypeStruct((depth, units), BF16),
            jax.ShapeDtypeStruct((units, depth), BF16),
        ],
        in_specs=[rows(depth, total), rows(units, total), whole(d_gate), whole(d_up), whole(grad)],
        out_specs=[rows(depth, units), rows(depth, units), rows(units, depth)],
        compiler_params=pltpu.CompilerParams(vmem_limit_bytes=62 * 2**20),
        cost_estimate=pl.CostEstimate(
            flops=6 * total * depth * units, bytes_accessed=6 * depth * units, transcendentals=0
        ),
        name="weight_grads",
    )(tok_t, hid_t, d_gate, d_up, grad)


def local(n, tokens, out_grad, gate_weight, up_weight, down_weight):
    tok_t, grad, hid_t, d_gate, d_up, pieces = forward(
        n, tokens, out_grad, gate_weight, up_weight, down_weight
    )
    arrived = lax.all_to_all(pieces, "col", 0, 0, tiled=True)
    grad_gate, grad_up, grad_down = weight_grads(tok_t, hid_t, d_gate, d_up, grad)
    grad_input = arrived[0].astype(F32)
    for k in range(1, n):
        grad_input = grad_input + arrived[k].astype(F32)
    return grad_input.astype(BF16), grad_gate, grad_up, grad_down


def solution(mesh):
    in_specs = (P("col", "row"), P("col", "row"), P("row", "col"), P("row", "col"), P("col", "row"))
    out_specs = (P("col", "row"), P("row", "col"), P("row", "col"), P("col", "row"))
    return jax.shard_map(
        functools.partial(local, mesh.shape["col"]),
        mesh=mesh, in_specs=in_specs, out_specs=out_specs, check_vma=False,
    )
```

```python
import functools

import jax
import jax.numpy as jnp
from jax import lax
from jax.experimental import pallas as pl
from jax.experimental.pallas import tpu as pltpu
from jax.sharding import PartitionSpec as P

MESH = pl.DeviceIdType.MESH
F32, BF16 = jnp.float32, jnp.bfloat16


def pointwise(gate, up, hidden_grad):
    logistic = jax.nn.sigmoid(gate)
    active = gate * logistic
    hidden = (active * up).astype(BF16)
    d_gate = (hidden_grad * up * logistic * (1.0 + gate * (1.0 - logistic))).astype(BF16)
    d_up = (hidden_grad * active).astype(BF16)
    return hidden, d_gate, d_up


def contract_last(left, right):
    return lax.dot_general(left, right, (((1,), (1,)), ((), ())), preferred_element_type=F32)


def chunk_width(units):
    for width in (512, 256, 128):
        if units % width == 0:
            return width
    return units


def loop(low, high, body):
    def step(index, carry):
        body(index)
        return carry

    lax.fori_loop(low, high, step, 0)


def forward_kernel(
    n, group, chunks, width,
    tokens, out_grad, gate_w, up_w, down_w,
    tok_out, grad_out, hid_out, dgate_out, dup_out, pieces_out,
    *scratch,
):
    (
        tok, grad, tok_t, hid_t, wg, wu, wd, part, core_in, x_send, x_in, res, acc,
        w_sem, own_sem, ag_send, ag_fwd, ag_recv,
        core_send_sem, core_recv_sem, x_send_sem, x_recv_sem, res_send_sem, res_recv_sem,
        out_sem, full_sem,
    ) = scratch
    block = tokens.shape[0]
    total = block * n
    half = total // 2
    row, me = lax.axis_index("row"), lax.axis_index("col")
    core = lax.rem(row, 2)
    core_peer = row + 1 - 2 * core
    x_peer = lax.rem(row + 2, 4)
    groups = n // group
    hi, lo = me // group, lax.rem(me, group)
    mine = pl.ds(pl.multiple_of(core * half, half), half)
    theirs = pl.ds(pl.multiple_of((1 - core) * half, half), half)

    def columns(c):
        return pl.ds(pl.multiple_of(c * width, width), width)

    def weight_copy(m, c):
        if m == 2:
            return pltpu.make_async_copy(
                down_w.at[columns(c), :], wd.at[columns(c), :], w_sem.at[m, c]
            )
        source, target = ((gate_w, wg), (up_w, wu))[m]
        return pltpu.make_async_copy(
            source.at[:, columns(c)], target.at[:, columns(c)], w_sem.at[m, c]
        )

    def load_pair(c):
        weight_copy(0, c).start()
        weight_copy(1, c).start()

    def place(owner):
        return pl.ds(pl.multiple_of(owner * block, block), block)

    def far(k):
        return lax.rem(hi + k, groups) * group + lo

    def far_from(k):
        return lax.rem(hi + groups - k, groups) * group + lo

    def near(j):
        return hi * group + lax.rem(lo + j, group)

    arrays = ((tokens, tok), (out_grad, grad))

    def own_copy(a):
        return pltpu.make_async_copy(arrays[a][0], arrays[a][1].at[place(me), :], own_sem.at[a])

    def own_send(a, peer):
        return pltpu.make_async_remote_copy(
            src_ref=arrays[a][0],
            dst_ref=arrays[a][1].at[place(me), :],
            send_sem=ag_send.at[a, peer],
            recv_sem=ag_recv.at[a, me],
            device_id={"col": peer},
            device_id_type=MESH,
        )

    def forward_send(a, owner, j):
        return pltpu.make_async_remote_copy(
            src_ref=arrays[a][1].at[place(owner), :],
            dst_ref=arrays[a][1].at[place(owner), :],
            send_sem=ag_fwd.at[a, owner, j],
            recv_sem=ag_recv.at[a, owner],
            device_id={"col": near(j)},
            device_id_type=MESH,
        )

    def wait_block(a, owner):
        pltpu.make_async_copy(
            arrays[a][0], arrays[a][1].at[place(owner), :], ag_recv.at[a, owner]
        ).wait()

    def gather_start(a):
        own_copy(a).start()
        loop(1, groups, lambda k: own_send(a, far(k)).start())
        loop(1, group, lambda j: own_send(a, near(j)).start())

    def gather_forward(a):
        def one(k):
            owner = far_from(k)
            wait_block(a, owner)
            loop(1, group, lambda j: forward_send(a, owner, j).start())

        loop(1, groups, one)

    def gather_finish(a):
        def one(j):
            peer = near(j)
            wait_block(a, peer)
            loop(1, groups, lambda k: wait_block(
                a, lax.rem(hi + groups - k, groups) * group + lax.rem(lo + j, group)))

        loop(1, group, one)
        own_copy(a).wait()

    def gather_drain(a):
        loop(1, groups, lambda k: own_send(a, far(k)).wait_send())
        loop(1, group, lambda j: own_send(a, near(j)).wait_send())
        loop(1, groups, lambda k: loop(
            1, group, lambda j: forward_send(a, far_from(k), j).wait_send()))

    def core_copy(m, c):
        return pltpu.make_async_remote_copy(
            src_ref=part.at[m, c, theirs, :],
            dst_ref=core_in.at[m, c],
            send_sem=core_send_sem.at[m, c],
            recv_sem=core_recv_sem.at[m, c],
            device_id={"row": core_peer},
            device_id_type=MESH,
        )

    def x_copy(m, c):
        return pltpu.make_async_remote_copy(
            src_ref=x_send.at[m, c],
            dst_ref=x_in.at[m, c],
            send_sem=x_send_sem.at[m, c],
            recv_sem=x_recv_sem.at[m, c],
            device_id={"row": x_peer},
            device_id_type=MESH,
        )

    def res_copy(c):
        return pltpu.make_async_remote_copy(
            src_ref=res.at[c, :, mine, :],
            dst_ref=res.at[c, :, mine, :],
            send_sem=res_send_sem.at[c],
            recv_sem=res_recv_sem.at[c],
            device_id={"row": core_peer},
            device_id_type=MESH,
        )

    def out_copy(k, c):
        if k == 0:
            return pltpu.make_async_copy(
                hid_t.at[columns(c), :], hid_out.at[columns(c), :], out_sem.at[k, c]
            )
        target = (dgate_out, dup_out)[k - 1]
        return pltpu.make_async_copy(res.at[c, k], target.at[:, columns(c)], out_sem.at[k, c])

    def multiply(m, c):
        weight_copy(m, c).wait()
        if m == 2:
            part[m, c] = contract_last(grad[...], wd[columns(c), :])
        else:
            weight = (wg, wu)[m]
            part[m, c] = jnp.dot(tok[...], weight[:, columns(c)], preferred_element_type=F32)
        core_copy(m, c).start()

    def chip_sum(m, c):
        core_copy(m, c).wait_recv()
        value = part[m, c, mine, :] + core_in[m, c]
        part[m, c, mine, :] = value
        x_send[m, c] = value.astype(BF16)
        x_copy(m, c).start()

    def gate_up(c):
        for m in range(2):
            multiply(m, c)

            @pl.when(c > 0)
            def _():
                chip_sum(m, c - 1)

    def down(c):
        multiply(2, c)

        @pl.when(c > 0)
        def _():
            chip_sum(2, c - 1)

    def later(c):
        multiply(0, c)

        @pl.when(c > early)
        def _():
            chip_sum(1, c - 1)

        multiply(1, c)
        chip_sum(2, c - 1)
        multiply(2, c)
        chip_sum(0, c)
        finish(c - early)

    def input_product(c):
        res_copy(c).wait_recv()
        out_copy(1, c).start()
        out_copy(2, c).start()
        hid_t[columns(c), :] = res[c, 0].T
        out_copy(0, c).start()
        acc[...] += contract_last(res[c, 1], wg[:, columns(c)])
        acc[...] += contract_last(res[c, 2], wu[:, columns(c)])

    def finish(c):
        for m in range(3):
            x_copy(m, c).wait_recv()
        values = [part[m, c, mine, :] + x_in[m, c].astype(F32) for m in range(3)]
        for k, value in enumerate(pointwise(*values)):
            res[c, k, mine, :] = value
        res_copy(c).start()

        @pl.when(c > 0)
        def _():
            input_product(c - 1)

    loop(0, chunks, load_pair)
    loop(0, chunks, lambda c: weight_copy(2, c).start())
    acc[...] = jnp.zeros_like(acc)

    barrier = pltpu.get_barrier_semaphore()
    loop(1, groups, lambda k: pl.semaphore_signal(
        barrier, inc=1, device_id={"col": far(k)}, device_id_type=MESH))
    loop(1, group, lambda j: pl.semaphore_signal(
        barrier, inc=1, device_id={"col": near(j)}, device_id_type=MESH))
    for peer in (core_peer, x_peer):
        pl.semaphore_signal(barrier, inc=1, device_id={"row": peer}, device_id_type=MESH)
    pl.semaphore_wait(barrier, groups + group)

    gather_start(0)
    gather_forward(0)
    gather_start(1)
    gather_finish(0)
    early = min(3, chunks)
    loop(0, early, gate_up)
    tok_t[...] = tok[...].T
    chip_sum(0, early - 1)
    chip_sum(1, early - 1)
    gather_forward(1)
    tok_copy = pltpu.make_async_copy(tok_t, tok_out, full_sem.at[0])
    tok_copy.start()
    gather_finish(1)
    grad_copy = pltpu.make_async_copy(grad, grad_out, full_sem.at[1])
    grad_copy.start()
    loop(0, early, down)
    loop(early, chunks, later)
    if chunks > early:
        chip_sum(1, chunks - 1)
    chip_sum(2, chunks - 1)
    loop(chunks - early, chunks, finish)
    input_product(chunks - 1)

    for k in range(n):
        pieces_out[k] = acc[k * block : (k + 1) * block, :].astype(BF16)

    gather_drain(0)
    gather_drain(1)

    def drain(c):
        for m in range(3):
            core_copy(m, c).wait_send()
            x_copy(m, c).wait_send()
            out_copy(m, c).wait()
        res_copy(c).wait_send()

    loop(0, chunks, drain)
    tok_copy.wait()
    grad_copy.wait()


def forward(n, tokens, out_grad, gate_w, up_w, down_w):
    block, depth = tokens.shape
    units = gate_w.shape[1]
    total = block * n
    width = chunk_width(units)
    chunks = units // width
    group = 2
    half = total // 2
    anywhere = pl.BlockSpec(memory_space=pl.ANY)
    inside = pl.BlockSpec(memory_space=pltpu.VMEM)
    full = jax.ShapeDtypeStruct((total, depth), BF16)
    hidden = jax.ShapeDtypeStruct((total, units), BF16)
    turned = jax.ShapeDtypeStruct((depth, total), BF16)
    hidden_t = jax.ShapeDtypeStruct((units, total), BF16)
    dma = pltpu.SemaphoreType.DMA
    return pl.pallas_call(
        functools.partial(forward_kernel, n, group, chunks, width),
        out_shape=[
            turned, full, hidden_t, hidden, hidden,
            jax.ShapeDtypeStruct((n, block, depth), BF16),
        ],
        in_specs=[anywhere] * 5,
        out_specs=[anywhere] * 5 + [inside],
        scratch_shapes=[
            pltpu.VMEM((total, depth), BF16),
            pltpu.VMEM((total, depth), BF16),
            pltpu.VMEM((depth, total), BF16),
            pltpu.VMEM((units, total), BF16),
            pltpu.VMEM((depth, units), BF16),
            pltpu.VMEM((depth, units), BF16),
            pltpu.VMEM((units, depth), BF16),
            pltpu.VMEM((3, chunks, total, width), F32),
            pltpu.VMEM((3, chunks, half, width), F32),
            pltpu.VMEM((3, chunks, half, width), BF16),
            pltpu.VMEM((3, chunks, half, width), BF16),
            pltpu.VMEM((chunks, 3, total, width), BF16),
            pltpu.VMEM((total, depth), F32),
            dma((3, chunks)),
            dma((2,)),
            dma((2, n)),
            dma((2, n, group)),
            dma((2, n)),
            dma((3, chunks)),
            dma((3, chunks)),
            dma((3, chunks)),
            dma((3, chunks)),
            dma((chunks,)),
            dma((chunks,)),
            dma((3, chunks)),
            dma((2,)),
        ],
        compiler_params=pltpu.CompilerParams(
            collective_id=0, has_side_effects=True, vmem_limit_bytes=63 * 2**20
        ),
        name="forward_exchange",
    )(tokens, out_grad, gate_w, up_w, down_w)


def grads_kernel(tok_t, hid_t, d_gate, d_up, grad, gate_o, up_o, down_o):
    for left, right, out in (
        (tok_t, d_gate, gate_o), (tok_t, d_up, up_o), (hid_t, grad, down_o)
    ):
        out[...] = jnp.dot(left[...], right[...], preferred_element_type=F32).astype(BF16)


def weight_grads(tok_t, hid_t, d_gate, d_up, grad):
    depth, total = tok_t.shape
    units = hid_t.shape[0]
    steps = max(s for s in (1, 2, 4, 8) if depth % (16 * s) == 0 and units % (16 * s) == 0)

    def rows(count, width):
        return pl.BlockSpec((count // steps, width), lambda i: (i, 0))

    def whole(array):
        return pl.BlockSpec(array.shape, lambda i: (0, 0))

    return pl.pallas_call(
        grads_kernel,
        grid=(steps,),
        out_shape=[
            jax.ShapeDtypeStruct((depth, units), BF16),
            jax.ShapeDtypeStruct((depth, units), BF16),
            jax.ShapeDtypeStruct((units, depth), BF16),
        ],
        in_specs=[rows(depth, total), rows(units, total), whole(d_gate), whole(d_up), whole(grad)],
        out_specs=[rows(depth, units), rows(depth, units), rows(units, depth)],
        compiler_params=pltpu.CompilerParams(vmem_limit_bytes=62 * 2**20),
        cost_estimate=pl.CostEstimate(
            flops=6 * total * depth * units, bytes_accessed=6 * depth * units, transcendentals=0
        ),
        name="weight_grads",
    )(tok_t, hid_t, d_gate, d_up, grad)


def local(n, tokens, out_grad, gate_weight, up_weight, down_weight):
    tok_t, grad, hid_t, d_gate, d_up, pieces = forward(
        n, tokens, out_grad, gate_weight, up_weight, down_weight
    )
    arrived = lax.all_to_all(pieces, "col", 0, 0, tiled=True)
    grad_gate, grad_up, grad_down = weight_grads(tok_t, hid_t, d_gate, d_up, grad)
    grad_input = arrived[0].astype(F32)
    for k in range(1, n):
        grad_input = grad_input + arrived[k].astype(F32)
    return grad_input.astype(BF16), grad_gate, grad_up, grad_down


def solution(mesh):
    in_specs = (P("col", "row"), P("col", "row"), P("row", "col"), P("row", "col"), P("col", "row"))
    out_specs = (P("col", "row"), P("row", "col"), P("row", "col"), P("col", "row"))
    return jax.shard_map(
        functools.partial(local, mesh.shape["col"]),
        mesh=mesh, in_specs=in_specs, out_specs=out_specs, check_vma=False,
    )
```
